32 devices in a mesh: dp: 2 (over x), expert: 16 (over z, y, core).
Axes of the slice: x: 2, y: 2, z: 4, core: 2. Of those that a mesh axis runs over, the one named last changes fastest.
Arguments:
- tokens: bfloat16 [64, 2048], P(('dp', 'expert')), may hold values from -6 to 6
- combine: bfloat16 [64], P(('dp', 'expert')), may hold values from 0.099609375 to 1
- routes: int32 [64], P(('dp', 'expert')), may hold values from 0 to 1, as said below
- capacity_slot: int32 [64], P(('dp', 'expert')), may hold values from -1 to 19, as said below
- readout: float32 [2048], replicated, may hold values from -6 to 6
- weight_in: bfloat16 [2, 2048, 14336], P('dp', None, 'expert'), may hold values from -0.125 to 0.125
- weight_out: bfloat16 [2, 14336, 2048], P('dp', 'expert'), may hold values from -0.046875 to 0.046875
Outputs:
- r2_grad: bfloat16 [64, 2048], P(('dp', 'expert'))
- grad_in: bfloat16 [2, 2048, 14336], P('dp', None, 'expert')
- grad_out: bfloat16 [2, 14336, 2048], P('dp', 'expert')
The draws below stay inside these ranges and needn't reach their ends.
Inputs may be any that keep to these rules, and one draw needn't show every extreme that they name: `routes`: each token's expert. `capacity_slot`: in each aligned block of 32 tokens, the tokens routed to one expert carry slots 0, 1, 2, ... in token order while fewer than 20 came before them, and -1 after; in every block some expert receives 30 tokens or more, so its 20 slots are full.
All inputs are finite; a program needn't handle non-finite values.
Results may differ from the reference program's by a relative error of at most 0.006.
Values may be sent and summed in bfloat16 or wider, within the bound.
No kernel may reach another device: no remote copies, remote signals or barrier semaphores. Data moves between devices by JAX's collectives and lax.ppermute only.
A program may use at most 64 MiB of HBM per device.

```python
import jax
import jax.numpy as jnp
from jax import lax

D = 2048
FF = 14336
GROUP_TOK = 32
TOKENS = 64
EXPERTS = 2
CAP = 20
HOT = 30
N_DP = 2


def route_plan(key):
    group_keys = jax.random.split(jax.random.fold_in(key, 7), N_DP)

    def one_group(group_key):
        hot_key, other_key, order_key = jax.random.split(group_key, 3)
        hot_expert = jax.random.randint(hot_key, (), 0, EXPERTS)
        others = jax.random.randint(other_key, (GROUP_TOK,), 0, EXPERTS)
        order_perm = jax.random.permutation(order_key, GROUP_TOK)
        marked = jnp.zeros((GROUP_TOK,), jnp.int32).at[order_perm[:HOT]].set(1)
        chosen = jnp.where(marked == 1, hot_expert, others).astype(jnp.int32)
        onehot = (chosen[:, None] == jnp.arange(EXPERTS, dtype=jnp.int32)[None, :]).astype(jnp.int32)
        before = jnp.cumsum(onehot, axis=0) - onehot
        rank_seen = jnp.sum(before * onehot, axis=1)
        slot_value = jnp.where(rank_seen < CAP, rank_seen, -1).astype(jnp.int32)
        return (chosen, slot_value)
    chosen, slot_value = jax.vmap(one_group)(group_keys)
    return (chosen.reshape(-1), slot_value.reshape(-1))


def draw_routes(key, part):
    return route_plan(key)[0]


def draw_capacity_slot(key, part):
    return route_plan(key)[1]


def block_scale(key, dims, pieces, smallest, top_value):
    factor_of = 1.0
    for axis_at, shards_of in pieces:
        steps = jax.random.uniform(jax.random.fold_in(jax.random.fold_in(key, 6), axis_at), (shards_of,), jnp.float32, smallest / len(pieces), top_value / len(pieces))
        factor_of = factor_of * jnp.repeat(jnp.exp(steps), dims[axis_at] // shards_of).reshape((-1,) + (1,) * (len(dims) - 1 - axis_at))
    return factor_of


def centred(own_key, shape, spread, most, shards=(), kind=jnp.bfloat16):
    drawn = jax.random.normal(own_key, shape, jnp.float32) * spread
    if len(shards) > 0:
        drawn = block_scale(own_key, shape, shards, -0.22, 0.18) * drawn
    return jnp.clip(drawn, min=-most, max=most).astype(kind)


def setup_inputs(seed: int = 0) -> dict:
    seeds = jax.random.split(jax.random.key(seed), 8)
    return {
        "tokens": centred(seeds[0], (TOKENS, D), 1.0, 6.0, ((0, 32),)),
        "combine": jnp.clip(0.099609375 + 0.9003906 * jax.random.uniform(seeds[1], (TOKENS,), jnp.float32) ** block_scale(seeds[1], (TOKENS,), ((0, 32),), -0.2, 0.2), 0.099609375, 1.0).astype(jnp.bfloat16),
        "routes": draw_routes(jax.random.fold_in(seeds[7], 71), 0),
        "capacity_slot": draw_capacity_slot(jax.random.fold_in(seeds[7], 71), 0),
        "readout": centred(seeds[4], (D,), 1.0, 6.0, (), jnp.float32),
        "weight_in": centred(seeds[5], (EXPERTS, D, FF), D ** -0.5, 0.125, ((0, 2), (2, 16))),
        "weight_out": centred(seeds[6], (EXPERTS, FF, D), FF ** -0.5, 0.046875, ((0, 2), (1, 16))),
    }


def expert_pass(rows_in, rows_c, readout, matrix_in, matrix_out):
    combine_col = rows_c.astype(jnp.float32)[:, None]
    head_row = readout[None, :]
    pre_act = jnp.dot(rows_in, matrix_in, preferred_element_type=jnp.float32)
    sigm = jax.nn.sigmoid(pre_act)
    slope_act = sigm * (1.0 + pre_act * (1.0 - sigm))
    bend_act = sigm * (1.0 - sigm) * (2.0 + pre_act * (1.0 - 2.0 * sigm))
    hidden = (pre_act * sigm).astype(jnp.bfloat16)
    mixed_sum = combine_col * jnp.dot(hidden, matrix_out, preferred_element_type=jnp.float32)
    tangent = jnp.tanh(rows_in.astype(jnp.float32) + mixed_sum)
    sech_sq = 1.0 - tangent * tangent
    upstream = head_row * sech_sq
    upstream_rows = upstream.astype(jnp.bfloat16)
    back_hidden = combine_col * jnp.dot(upstream_rows, matrix_out.T, preferred_element_type=jnp.float32)
    back_pre = (back_hidden * slope_act).astype(jnp.bfloat16)
    grad_rows = (upstream + jnp.dot(back_pre, matrix_in.T, preferred_element_type=jnp.float32)).astype(jnp.bfloat16)
    second = jnp.dot(grad_rows, matrix_in, preferred_element_type=jnp.float32)
    push_rows = (combine_col * second * slope_act).astype(jnp.bfloat16)
    total_push = grad_rows.astype(jnp.float32) + jnp.dot(push_rows, matrix_out, preferred_element_type=jnp.float32)
    curve_term = total_push * head_row * (-2.0 * tangent * sech_sq)
    echo_rows = (combine_col * curve_term).astype(jnp.bfloat16)
    back_second = jnp.dot(echo_rows, matrix_out.T, preferred_element_type=jnp.float32)
    final_pre = (back_second * slope_act + second * back_hidden * bend_act).astype(jnp.bfloat16)
    grad_in = (jnp.dot(grad_rows.T, back_pre, preferred_element_type=jnp.float32)
               + jnp.dot(rows_in.T, final_pre, preferred_element_type=jnp.float32)).astype(jnp.bfloat16)
    grad_out = (jnp.dot(push_rows.T, upstream_rows, preferred_element_type=jnp.float32)
                + jnp.dot(hidden.T, echo_rows, preferred_element_type=jnp.float32)).astype(jnp.bfloat16)
    return grad_rows, grad_in, grad_out


def reference(tokens, combine, routes, capacity_slot, readout, weight_in, weight_out):
    slot_total = EXPERTS * CAP
    grouped = tokens.reshape(N_DP, GROUP_TOK, D).astype(jnp.float32)
    grouped_c = combine.reshape(N_DP, GROUP_TOK).astype(jnp.float32)
    slot_place = (routes * CAP + capacity_slot).astype(jnp.int32).reshape(N_DP, GROUP_TOK)
    kept = (capacity_slot >= 0).reshape(N_DP, GROUP_TOK)
    slot_index = jnp.arange(slot_total, dtype=jnp.int32)
    onehot = ((slot_index[None, :, None] == slot_place[:, None, :]) & kept[:, None, :]).astype(jnp.float32)
    packed = jnp.einsum("rst,rtd->rsd", onehot, grouped).astype(jnp.bfloat16)
    packed_c = jnp.einsum("rst,rt->rs", onehot, grouped_c).astype(jnp.bfloat16)
    per_expert = packed.reshape(N_DP, EXPERTS, CAP, D).transpose(1, 0, 2, 3).reshape(EXPERTS, N_DP * CAP, D)
    per_expert_c = packed_c.reshape(N_DP, EXPERTS, CAP).transpose(1, 0, 2).reshape(EXPERTS, N_DP * CAP)

    def one_expert(operands):
        return expert_pass(operands[0], operands[1], readout, operands[2], operands[3])

    grad_rows, grad_in, grad_out = lax.map(one_expert, (per_expert, per_expert_c, weight_in, weight_out))
    home_rows = grad_rows.reshape(EXPERTS, N_DP, CAP, D).transpose(1, 0, 2, 3).reshape(N_DP, slot_total, D)
    clipped = jnp.clip(slot_place, 0, slot_total - 1).astype(jnp.int32)
    picked = jax.vmap(lambda rows, where_at: jnp.take(rows, where_at, axis=0))(home_rows, clipped)
    picked = picked.reshape(TOKENS, D)
    tangent_home = jnp.tanh(tokens.astype(jnp.float32))
    dropped = (readout[None, :] * (1.0 - tangent_home * tangent_home)).astype(jnp.bfloat16)
    r2_grad = jnp.where((capacity_slot >= 0)[:, None], picked, dropped)
    return r2_grad, grad_in, grad_out
```

```python
import jax
import jax.numpy as jnp
from jax import lax
from jax.sharding import PartitionSpec as P

BF = jnp.bfloat16
F32 = jnp.float32


def contract_rows(left, right):
    return lax.dot_general(left, right, (((0,), (0,)), ((), ())), preferred_element_type=F32)


def contract_cols(left, right):
    return lax.dot_general(left, right, (((1,), (1,)), ((), ())), preferred_element_type=F32)


def dot(left, right):
    return jnp.dot(left, right, preferred_element_type=F32)


def digits(total):
    sizes = []
    rest = total
    if rest % 2 == 0:
        sizes.append(2)
        rest //= 2
    twos = 0
    while rest % 2 == 0:
        rest //= 2
        twos += 1
    sizes += [2] * (twos % 2) + [4] * (twos // 2)
    if rest > 1:
        sizes.append(rest)
    placed, stride = [], 1
    for size in sizes:
        placed.append((stride, size))
        stride *= size
    return placed


def moved(index, stride, size, offset):
    digit = (index // stride) % size
    if size & (size - 1) == 0:
        target = digit ^ offset
    else:
        target = (digit + offset) % size
    return index + (target - digit) * stride


def fetch(values, axis, stride, size, offset, back=False):
    total = lax.axis_size(axis)
    pairs = [(moved(i, stride, size, offset), i) for i in range(total)]
    if back:
        pairs = [(there, here) for here, there in pairs]
    return lax.ppermute(values, axis, pairs)


def gather_rows(values, axis, stride, size):
    parts = [values] + [fetch(values, axis, stride, size, k) for k in range(1, size)]
    return jnp.concatenate(parts, axis=0)


def shards(tokens, combine, routes, capacity_slot, readout, weight_in, weight_out):
    n_dp = lax.axis_size("dp")
    n_ex = lax.axis_size("expert")
    local, width = tokens.shape
    capacity = 5 * local * n_ex // (4 * n_dp)
    rows = n_dp * capacity
    me_dp = lax.axis_index("dp")
    splits = digits(n_ex)
    core, chips = splits[0], splits[1:]

    kept = capacity_slot >= 0
    place = jnp.where(kept, me_dp * capacity + capacity_slot, -1)
    expert_id = jnp.where(kept, routes, -1)
    meta = jnp.stack(
        [expert_id.astype(BF), (place // 128).astype(BF), (place % 128).astype(BF), combine],
        axis=1,
    )
    packed = jnp.concatenate([tokens, jnp.pad(meta, ((0, 0), (0, 124)))], axis=1)

    gathered = gather_rows(packed, "dp", 1, n_dp)
    for stride, size in chips + [core]:
        gathered = gather_rows(gathered, "expert", stride, size)

    all_meta = gathered[:, width:].astype(F32)
    all_expert = all_meta[:, 0].astype(jnp.int32)
    all_place = (all_meta[:, 1] * 128 + all_meta[:, 2]).astype(jnp.int32)
    row_of = jnp.where(all_expert == me_dp, all_place, -1)
    onehot = (lax.iota(jnp.int32, rows)[:, None] == row_of[None, :]).astype(BF)
    rows_all = dot(onehot, gathered).astype(BF)
    rows_in = rows_all[:, :width]
    combine_col = rows_all[:, width + 3 : width + 4].astype(F32)

    matrix_in = weight_in[0]
    matrix_out = weight_out[0]
    half = width // core[1]
    my_core = lax.axis_index("expert") % core[1]
    head_part = lax.dynamic_slice_in_dim(readout[None, :], my_core * half, half, 1)

    def core_part(values, offset):
        at = moved(my_core, 1, core[1], offset)
        return lax.dynamic_slice_in_dim(values, at * half, half, 1)

    def shared_sum(term):
        total = core_part(term, 0)
        for k in range(1, core[1]):
            total = total + fetch(core_part(term, k), "expert", *core, k, back=False)
        for stride, size in chips:
            own = total.astype(BF)
            parts = [own] + [fetch(own, "expert", stride, size, k) for k in range(1, size)]
            total = sum(part.astype(F32) for part in parts)
        return total

    def regather(values):
        full = jnp.zeros((values.shape[0], width), values.dtype)
        for k in range(core[1]):
            part = values if k == 0 else fetch(values, "expert", *core, k)
            at = moved(my_core, 1, core[1], k)
            full = lax.dynamic_update_slice_in_dim(full, part, at * half, 1)
        return full

    pre_act = dot(rows_in, matrix_in)
    sigm = jax.nn.sigmoid(pre_act)
    slope_act = sigm * (1.0 + pre_act * (1.0 - sigm))
    bend_act = sigm * (1.0 - sigm) * (2.0 + pre_act * (1.0 - 2.0 * sigm))
    hidden = (pre_act * sigm).astype(BF)
    mixed = shared_sum(combine_col * dot(hidden, matrix_out))
    tangent = jnp.tanh(core_part(rows_in, 0).astype(F32) + mixed)
    sech_sq = 1.0 - tangent * tangent
    upstream = head_part * sech_sq
    upstream_rows = regather(upstream.astype(BF))
    back_hidden = combine_col * contract_cols(upstream_rows, matrix_out)
    back_pre = (back_hidden * slope_act).astype(BF)
    grad_part = (upstream + shared_sum(contract_cols(back_pre, matrix_in))).astype(BF)
    grad_rows = regather(grad_part)
    second = dot(grad_rows, matrix_in)
    push_rows = (combine_col * second * slope_act).astype(BF)
    total_push = grad_part.astype(F32) + shared_sum(dot(push_rows, matrix_out))
    curve_term = total_push * head_part * (-2.0 * tangent * sech_sq)
    echo_rows = regather((combine_col * curve_term).astype(BF))
    back_second = contract_cols(echo_rows, matrix_out)
    final_pre = (back_second * slope_act + second * back_hidden * bend_act).astype(BF)
    grad_in = contract_rows(
        jnp.concatenate([grad_rows, rows_in], 0), jnp.concatenate([back_pre, final_pre], 0)
    ).astype(BF)
    grad_out = contract_rows(
        jnp.concatenate([push_rows, hidden], 0), jnp.concatenate([upstream_rows, echo_rows], 0)
    ).astype(BF)

    picked = jnp.zeros((local, width), F32)
    for k in range(n_dp):
        rows_wanted = row_of[k * local : (k + 1) * local]
        pick = (rows_wanted[:, None] == lax.iota(jnp.int32, rows)[None, :]).astype(BF)
        found = dot(pick, grad_rows).astype(BF)
        if k > 0:
            found = fetch(found, "dp", 1, n_dp, k, back=True)
        picked = picked + found.astype(F32)
    tangent_home = jnp.tanh(tokens.astype(F32))
    dropped = readout[None, :] * (1.0 - tangent_home * tangent_home)
    r2_grad = jnp.where(kept[:, None], picked, dropped).astype(BF)
    return (r2_grad, grad_in[None], grad_out[None])


def solution(mesh):
    placed = (
        P(("dp", "expert"), None),
        P(("dp", "expert")),
        P(("dp", "expert")),
        P(("dp", "expert")),
        P(),
        P("dp", None, "expert"),
        P("dp", "expert", None),
    )
    return jax.shard_map(
        shards,
        mesh=mesh,
        in_specs=placed,
        out_specs=(P(("dp", "expert"), None), P("dp", None, "expert"), P("dp", "expert", None)),
        check_vma=False,
    )
```

```python
import functools
import itertools

import jax
import jax.numpy as jnp
from jax import lax
from jax.experimental import pallas as pl
from jax.experimental.pallas import tpu as pltpu
from jax.sharding import PartitionSpec as P

BF = jnp.bfloat16
F32 = jnp.float32


def contract_rows(left, right):
    return lax.dot_general(left, right, (((0,), (0,)), ((), ())), preferred_element_type=F32)


def contract_cols(left, right):
    return lax.dot_general(left, right, (((1,), (1,)), ((), ())), preferred_element_type=F32)


def dot(left, right):
    return jnp.dot(left, right, preferred_element_type=F32)


def digits(total):
    sizes = []
    rest = total
    if rest % 2 == 0:
        sizes.append(2)
        rest //= 2
    twos = 0
    while rest % 2 == 0:
        rest //= 2
        twos += 1
    sizes += [2] * (twos % 2) + [4] * (twos // 2)
    if rest > 1:
        sizes.append(rest)
    placed, stride = [], 1
    for size in sizes:
        placed.append((stride, size))
        stride *= size
    return placed


def moved(index, stride, size, offset):
    digit = (index // stride) % size
    if size & (size - 1) == 0:
        target = digit ^ offset
    else:
        target = (digit + offset) % size
    return index + (target - digit) * stride


def fetch(values, steps, back=False):
    axes = ("dp", "expert")
    pairs = []
    for here in range(lax.axis_size(axes)):
        there = here
        for stride, size, offset in steps:
            there = moved(there, stride, size, offset)
        pairs.append((here, there) if back else (there, here))
    return lax.ppermute(values, axes, pairs)


def offsets_of(stage):
    return list(itertools.product(*[range(size) for _, size in stage]))


def steps_of(stage, offset):
    return [(*digit, k) for digit, k in zip(stage, offset) if k > 0]


def gather_rows(values, stages, hold_first, hold_second):
    held, blocks, kept = [values], [()], [hold_first(values)]
    for at, stage in enumerate(stages):
        offsets = offsets_of(stage)
        if at == 1:
            held[0] = lax.optimization_barrier(held[0] + kept[0][1])
        if held[0].shape[0] < 8:
            held = [jnp.concatenate(held, axis=0)]
        if at == 1:
            kept.append(hold_second(held[0]))
        if at > 1 and at == len(stages) - 1:
            held[0] = held[0] + kept[1][1]
        held += [fetch(part, steps_of(stage, offset)) for offset in offsets[1:] for part in held]
        blocks = [block + tuple(steps_of(stage, offset)) for offset in offsets for block in blocks]
    return held, blocks, [first for first, _ in kept]


def chunks(total, step):
    return [(at, min(step, total - at)) for at in range(0, total, step)]


def padded(rows):
    return -(-rows // 16) * 16


def stack(ref, low, high, columns=slice(None)):
    rows = low.shape[0]
    space = padded(rows)
    for at, values in ((0, low), (space, high)):
        if space > rows:
            fill = jnp.zeros((space - rows, values.shape[1]), values.dtype)
            values = jnp.concatenate([values, fill], axis=0)
        ref[at : at + space, columns] = values


def own_and_other(size):
    core = lax.rem(lax.axis_index("expert"), 2)
    return tuple(pl.ds(pl.multiple_of(at * size, size), size) for at in (core, 1 - core))


def forward_kernel(local, found_at, capacity, *refs):
    *parts, w_in, w_out, rows_in, col, col_wide, hidden, slope, bend, mine, other, picks = refs
    rows, width = rows_in.shape
    gathered = jnp.concatenate([part[...] for part in parts], axis=0)
    meta = gathered[:, width:].astype(F32)
    me = lax.axis_index("dp").astype(F32)
    slot = meta[:, 1:2] * 128.0 + meta[:, 2:3]
    place = jnp.where(meta[:, 0:1] == me, meta[:, 4:5] * float(capacity) + slot, -1.0)
    place = jnp.where(slot >= 0.0, place, -1.0)
    wanted = lax.broadcasted_iota(jnp.int32, (meta.shape[0], rows), 1).astype(F32)
    onehot = (place == wanted).astype(F32)
    found = contract_rows(onehot.astype(BF), gathered)
    packed_rows = found[:, :width].astype(BF)
    weight = found[:, width + 3 : width + 4]
    rows_in[...] = packed_rows
    picks[...] = jnp.concatenate([onehot[at : at + local] for at in found_at], axis=0)
    col[...] = weight
    col_wide[...] = jnp.broadcast_to(weight, col_wide.shape)
    pre = dot(packed_rows, w_in[...])
    sigm = jax.nn.sigmoid(pre)
    slope[...] = sigm * (1.0 + pre * (1.0 - sigm))
    bend[...] = sigm * (1.0 - sigm) * (2.0 + pre * (1.0 - 2.0 * sigm))
    act = (pre * sigm).astype(BF)
    hidden[...] = act
    at_own, at_other = own_and_other(width // 2)
    other[...] = weight * dot(act, w_out[:, at_other])
    mine[...] = weight * dot(act, w_out[:, at_own])


def backward_kernel(up_own, up_other, col, slope, w_in, w_out, back_hidden, back_pre, mine, other):
    at_own, at_other = own_and_other(up_own.shape[1])
    back = contract_cols(up_own[...], w_out[:, at_own])
    back += contract_cols(up_other[...], w_out[:, at_other])
    back = col[...] * back
    back_hidden[...] = back
    back = (back * slope[...]).astype(BF)
    back_pre[...] = back
    other[...] = contract_cols(back, w_in[at_other, :])
    mine[...] = contract_cols(back, w_in[at_own, :])


def push_kernel(grad_own, grad_other, col, slope, picks, w_in, w_out, second, push, mine, other, *home):
    half = grad_own.shape[1]
    at_own, at_other = own_and_other(half)
    pick = picks[...].astype(BF)
    local = home[0].shape[0]
    for columns, grad in ((slice(0, half), grad_own), (slice(half, 2 * half), grad_other)):
        found = dot(pick, grad[...])
        for k, result in enumerate(home):
            result[:, columns] = found[k * local : (k + 1) * local].astype(BF)
    moved_rows = dot(grad_own[...], w_in[at_own, :]) + dot(grad_other[...], w_in[at_other, :])
    second[...] = moved_rows
    moved_rows = (col[...] * moved_rows * slope[...]).astype(BF)
    push[...] = moved_rows
    other[...] = dot(moved_rows, w_out[:, at_other])
    mine[...] = dot(moved_rows, w_out[:, at_own])


def final_kernel(
    echo_own, echo_other, up_own, up_other, grad_own, grad_other, rows_in, push, hidden, back_pre,
    slope, bend, second, back_hidden, w_out, grad_in, grad_out,
    left_out, right_out, left_in, right_in, made_in, made_out, sem_in, sem_out,
):
    ranges = own_and_other(echo_own.shape[1])
    stack(left_out, push[...], hidden[...])
    for at, up, echo in zip(ranges, (up_own, up_other), (echo_own, echo_other)):
        stack(right_out, up[...], echo[...], at)
    copies = []

    def product(left, right, made, result, sem, step):
        for i, (at, size) in enumerate(chunks(left.shape[1], step)):
            made[at : at + size, :] = contract_rows(left[:, at : at + size], right[...]).astype(BF)
            part = pl.ds(at, size)
            copy = pltpu.make_async_copy(made.at[part], result.at[part], sem.at[i])
            copy.start()
            copies.append(copy)

    product(left_out, right_out, made_out, grad_out, sem_out, 128)
    back = contract_cols(echo_own[...], w_out[:, ranges[0]])
    back += contract_cols(echo_other[...], w_out[:, ranges[1]])
    final_pre = (back * slope[...] + second[...] * back_hidden[...] * bend[...]).astype(BF)
    stack(right_in, back_pre[...], final_pre)
    rows = rows_in[...]
    for at, grad in zip(ranges, (grad_own, grad_other)):
        left_in[0 : grad.shape[0], at] = grad[...]
    if padded(rows.shape[0]) > rows.shape[0]:
        fill = jnp.zeros((padded(rows.shape[0]) - rows.shape[0], rows.shape[1]), BF)
        left_in[rows.shape[0] : padded(rows.shape[0]), :] = fill
        rows = jnp.concatenate([rows, fill], axis=0)
    left_in[rows.shape[0] :, :] = rows
    product(left_in, right_in, made_in, grad_in, sem_in, 256)
    for copy in copies:
        copy.wait()


def run(kernel, shapes, args, scratch=(), flops=0, hbm=False):
    space = pl.ANY if hbm else pltpu.VMEM
    return pl.pallas_call(
        kernel,
        out_shape=[jax.ShapeDtypeStruct(shape, kind) for shape, kind in shapes],
        in_specs=[pl.BlockSpec(memory_space=pltpu.VMEM)] * len(args),
        out_specs=[pl.BlockSpec(memory_space=space)] * len(shapes),
        scratch_shapes=list(scratch),
        compiler_params=pltpu.CompilerParams(vmem_limit_bytes=20 << 20),
        cost_estimate=pl.CostEstimate(flops=flops, bytes_accessed=0, transcendentals=0),
    )(*[pltpu.with_memory_space_constraint(arg, pltpu.VMEM) for arg in args])


def hold(matrix, after):
    def kernel(source, after_ref, held, there, sem):
        del after_ref
        copy = pltpu.make_async_copy(source, held, sem)
        copy.start()
        there[...] = jnp.zeros_like(there)
        copy.wait()

    vmem = pl.BlockSpec(memory_space=pltpu.VMEM)
    return pl.pallas_call(
        kernel,
        out_shape=(pltpu.VMEM(matrix.shape, matrix.dtype), pltpu.VMEM(after.shape, BF)),
        in_specs=[pl.BlockSpec(memory_space=pltpu.HBM), pl.BlockSpec(memory_space=pl.ANY)],
        out_specs=(vmem, vmem),
        scratch_shapes=[pltpu.SemaphoreType.DMA],
        compiler_params=pltpu.CompilerParams(vmem_limit_bytes=1 << 20),
        cost_estimate=pl.CostEstimate(flops=0, bytes_accessed=matrix.size * 4, transcendentals=0),
    )(pltpu.with_memory_space_constraint(matrix, pltpu.HBM), after)


def pack(tokens, combine, routes, capacity_slot):
    local, width = tokens.shape
    shape = (local, width + 128)
    column = lax.broadcasted_iota(jnp.int32, shape, 1) - width
    routes, slots, combine = (
        lax.broadcast_in_dim(values, shape, (0,)) for values in (routes, capacity_slot, combine)
    )
    numbers = jnp.where(column == 4, lax.axis_index("dp"), slots & 127)
    numbers = jnp.where(column == 1, slots >> 7, numbers)
    numbers = jnp.where(column == 0, routes, numbers).astype(BF)
    numbers = jnp.where(column == 3, combine, numbers)
    return jnp.where(column < 0, jnp.pad(tokens, ((0, 0), (0, 128))), numbers)


def shards(tokens, combine, routes, capacity_slot, readout, weight_in, weight_out):
    n_dp = lax.axis_size("dp")
    n_ex = lax.axis_size("expert")
    local, width = tokens.shape
    units = weight_in.shape[2]
    capacity = 5 * local * n_ex // (4 * n_dp)
    rows = n_dp * capacity
    splits = digits(n_ex)
    core, chips = splits[0], splits[1:]

    kept = capacity_slot >= 0
    packed = pack(tokens, combine, routes, capacity_slot)
    first_core = lax.axis_index("expert") % core[1] == 0
    packed, first_core = lax.optimization_barrier((packed, first_core))

    dp_digit = (n_ex, n_dp)
    if n_dp * chips[0][1] <= 4:
        stages = [[dp_digit, chips[0]]] + [[digit] for digit in chips[1:]]
    else:
        stages = [[dp_digit]] + [[digit] for digit in chips]
    stages += [[core]]
    gathered, blocks, (matrix_in, matrix_out) = gather_rows(
        packed,
        stages,
        functools.partial(hold, weight_in[0]),
        functools.partial(hold, weight_out[0]),
    )
    found_at = [blocks.index(((*dp_digit, k),) if k > 0 else ()) * local for k in range(n_dp)]

    half = width // 2
    head_part = jnp.where(first_core, readout[None, :half], readout[None, half:])
    wide, thin, part = (rows, width), (rows, units), (rows, half)
    flops = 4 * rows * width * units

    def swap(values):
        return fetch(values, [(*core, 1)])

    def shared_sum(mine, other):
        total = mine + swap(other)
        for digit in chips:
            own = total.astype(BF)
            parts = [own] + [fetch(own, [(*digit, k)]) for k in range(1, digit[1])]
            total = sum(part.astype(F32) for part in parts)
        return total

    rows_in, col, col_wide, hidden, slope, bend, mine, other, picks = run(
        functools.partial(forward_kernel, local, found_at, capacity),
        [(wide, BF), ((rows, 1), F32), (part, F32), (thin, BF), (thin, F32), (thin, F32),
         (part, F32), (part, F32), ((n_dp * local, rows), F32)],
        (*gathered, matrix_in, matrix_out),
        flops=flops,
    )
    mixed = shared_sum(mine, other)
    rows_part = jnp.where(first_core, rows_in[:, :half], rows_in[:, half:])
    tangent = jnp.tanh(rows_part.astype(F32) + mixed)
    sech_sq = 1.0 - tangent * tangent
    upstream = head_part * sech_sq
    up_own = upstream.astype(BF)
    up_other = swap(up_own)
    back_hidden, back_pre, mine, other = run(
        backward_kernel,
        [(thin, F32), (thin, BF), (part, F32), (part, F32)],
        (up_own, up_other, col, slope, matrix_in, matrix_out),
        flops=flops,
    )
    grad_own = (upstream + shared_sum(mine, other)).astype(BF)
    grad_other = swap(grad_own)
    second, push, mine, other, *home = run(
        push_kernel,
        [(thin, F32), (thin, BF), (part, F32), (part, F32)] + [((local, width), BF)] * n_dp,
        (grad_own, grad_other, col, slope, picks, matrix_in, matrix_out),
        flops=flops,
    )
    total_push = grad_own.astype(F32) + shared_sum(mine, other)
    curve_term = total_push * head_part * (-2.0 * tangent * sech_sq)
    echo_own = (col_wide * curve_term).astype(BF)
    echo_other = swap(echo_own)
    deep = 2 * padded(rows)
    grad_in, grad_out = run(
        final_kernel,
        [((width, units), BF), ((units, width), BF)],
        (echo_own, echo_other, up_own, up_other, grad_own, grad_other, rows_in, push, hidden,
         back_pre, slope, bend, second, back_hidden, matrix_out),
        scratch=[
            pltpu.VMEM((deep, units), BF),
            pltpu.VMEM((deep, width), BF),
            pltpu.VMEM((deep, width), BF),
            pltpu.VMEM((deep, units), BF),
            pltpu.VMEM((width, units), BF),
            pltpu.VMEM((units, width), BF),
            pltpu.SemaphoreType.DMA((len(chunks(width, 256)),)),
            pltpu.SemaphoreType.DMA((len(chunks(units, 128)),)),
        ],
        flops=flops,
        hbm=True,
    )

    picked = home[0].astype(F32)
    for k in range(1, n_dp):
        picked = picked + fetch(home[k], [(*dp_digit, k)], back=True).astype(F32)
    swapped = jnp.concatenate([picked[:, half:], picked[:, :half]], 1)
    picked = jnp.where(first_core, picked, swapped)
    tangent_home = jnp.tanh(tokens.astype(F32))
    dropped = readout[None, :] * (1.0 - tangent_home * tangent_home)
    r2_grad = jnp.where(kept[:, None], picked, dropped).astype(BF)
    return (r2_grad, grad_in[None], grad_out[None])


def solution(mesh):
    placed = (
        P(("dp", "expert"), None),
        P(("dp", "expert")),
        P(("dp", "expert")),
        P(("dp", "expert")),
        P(),
        P("dp", None, "expert"),
        P("dp", "expert", None),
    )
    return jax.shard_map(
        shards,
        mesh=mesh,
        in_specs=placed,
        out_specs=(P(("dp", "expert"), None), P("dp", None, "expert"), P("dp", "expert", None)),
        check_vma=False,
    )
```

```python
import functools
import itertools

import jax
import jax.numpy as jnp
from jax import lax
from jax.experimental import pallas as pl
from jax.experimental.pallas import tpu as pltpu
from jax.sharding import PartitionSpec as P

BF = jnp.bfloat16
F32 = jnp.float32


def contract_rows(left, right):
    return lax.dot_general(left, right, (((0,), (0,)), ((), ())), preferred_element_type=F32)


def contract_cols(left, right):
    return lax.dot_general(left, right, (((1,), (1,)), ((), ())), preferred_element_type=F32)


def dot(left, right):
    return jnp.dot(left, right, preferred_element_type=F32)


def digits(total):
    placed, stride = [], 1
    while stride < total:
        size = 2 if total // stride % 2 == 0 else total // stride
        placed.append((stride, size))
        stride *= size
    return placed


def pairs(some):
    return [some[at : at + 2] for at in range(0, len(some), 2)]


def moved(index, stride, size, offset):
    digit = (index // stride) % size
    if size & (size - 1) == 0:
        target = digit ^ offset
    else:
        target = (digit + offset) % size
    return index + (target - digit) * stride


def fetch(values, steps, back=False):
    axes = ("dp", "expert")
    pairs = []
    for here in range(lax.axis_size(axes)):
        there = here
        for stride, size, offset in steps:
            there = moved(there, stride, size, offset)
        pairs.append((here, there) if back else (there, here))
    return lax.ppermute(values, axes, pairs)


def offsets_of(stage):
    return list(itertools.product(*[range(size) for _, size in stage]))


def steps_of(stage, offset):
    return [(*digit, k) for digit, k in zip(stage, offset) if k > 0]


def gather_rows(values, stages, hold_first, hold_second):
    held, blocks, kept = [values], [()], [hold_first(values)]
    for at, stage in enumerate(stages):
        offsets = offsets_of(stage)
        if at == 1:
            held[0] = lax.optimization_barrier(held[0] + kept[0][1])
        if held[0].shape[0] < 8:
            held = [jnp.concatenate(held, axis=0)]
        if at == 1:
            kept.append(hold_second(held[0]))
        if at > 1 and at == len(stages) - 1:
            held[0] = held[0] + kept[1][1]
        held += [fetch(part, steps_of(stage, offset)) for offset in offsets[1:] for part in held]
        blocks = [block + tuple(steps_of(stage, offset)) for offset in offsets for block in blocks]
    return held, blocks, [first for first, _ in kept]


def chunks(total, step):
    return [(at, min(step, total - at)) for at in range(0, total, step)]


def padded(rows):
    return -(-rows // 16) * 16


def stack(ref, low, high, columns=slice(None)):
    rows = low.shape[0]
    space = padded(rows)
    for at, values in ((0, low), (space, high)):
        if space > rows:
            fill = jnp.zeros((space - rows, values.shape[1]), values.dtype)
            values = jnp.concatenate([values, fill], axis=0)
        ref[at : at + space, columns] = values


def own_and_other(size):
    core = lax.rem(lax.axis_index("expert"), 2)
    return tuple(pl.ds(pl.multiple_of(at * size, size), size) for at in (core, 1 - core))


def forward_kernel(local, found_at, *refs):
    *parts, w_in, w_out, rows_in, col, hidden, pre_act, other, picks = refs
    rows, width = rows_in.shape
    gathered = jnp.concatenate([part[...] for part in parts], axis=0)
    meta = gathered[:, width:].astype(F32)
    me = lax.axis_index("dp").astype(F32)
    slot = meta[:, 1:2] * 128.0 + meta[:, 2:3]
    capacity = float(rows // lax.axis_size("dp"))
    place = jnp.where(meta[:, 0:1] == me, meta[:, 4:5] * capacity + slot, -1.0)
    place = jnp.where(slot >= 0.0, place, -1.0)
    wanted = lax.broadcasted_iota(jnp.int32, (meta.shape[0], rows), 1).astype(F32)
    onehot = (place == wanted).astype(F32)
    found = contract_rows(onehot.astype(BF), gathered)
    packed_rows = found[:, :width].astype(BF)
    weight = found[:, width + 3 : width + 4]
    rows_in[...] = packed_rows
    picks[...] = jnp.concatenate([onehot[at : at + local] for at in found_at], axis=0)
    col[...] = weight
    pre = dot(packed_rows, w_in[...])
    pre_act[...] = pre
    act = (pre * jax.nn.sigmoid(pre)).astype(BF)
    hidden[...] = act
    other[...] = (weight * dot(act, w_out[:, own_and_other(width // 2)[1]])).astype(BF)


def mix_kernel(hidden, pre_act, col, w_out, mine, slope, bend, col_wide):
    mine[...] = col[...] * dot(hidden[...], w_out[:, own_and_other(mine.shape[1])[0]])
    pre = pre_act[...]
    sigm = jax.nn.sigmoid(pre)
    slope[...] = sigm * (1.0 + pre * (1.0 - sigm))
    bend[...] = sigm * (1.0 - sigm) * (2.0 + pre * (1.0 - 2.0 * sigm))
    col_wide[...] = jnp.broadcast_to(col[...], col_wide.shape)


def back_own_kernel(up_own, w_out, back_own):
    back_own[...] = contract_cols(up_own[...], w_out[:, own_and_other(up_own.shape[1])[0]])


def backward_kernel(back_own, up_other, col, slope, w_in, w_out, back_hidden, back_pre, other):
    at_other = own_and_other(up_other.shape[1])[1]
    back = col[...] * (back_own[...] + contract_cols(up_other[...], w_out[:, at_other]))
    back_hidden[...] = back
    back = (back * slope[...]).astype(BF)
    back_pre[...] = back
    other[...] = contract_cols(back, w_in[at_other, :]).astype(BF)


def grad_kernel(back_pre, w_in, mine):
    mine[...] = contract_cols(back_pre[...], w_in[own_and_other(mine.shape[1])[0], :])


def second_own_kernel(grad_own, w_in, second_own):
    second_own[...] = dot(grad_own[...], w_in[own_and_other(grad_own.shape[1])[0], :])


def push_kernel(second_own, grad_other, col, slope, w_in, w_out, second, push, other):
    at_other = own_and_other(grad_other.shape[1])[1]
    moved_rows = second_own[...] + dot(grad_other[...], w_in[at_other, :])
    second[...] = moved_rows
    moved_rows = (col[...] * moved_rows * slope[...]).astype(BF)
    push[...] = moved_rows
    other[...] = dot(moved_rows, w_out[:, at_other]).astype(BF)


def pull_kernel(
    push, hidden, grad_own, grad_other, rows_in, picks, w_out, mine, left_out, left_in, *home
):
    half = mine.shape[1]
    mine[...] = dot(push[...], w_out[:, own_and_other(half)[0]])
    pick = picks[...].astype(BF)
    local = home[0].shape[0]
    for columns, grad in ((slice(0, half), grad_own), (slice(half, 2 * half), grad_other)):
        found = dot(pick, grad[...])
        for k, result in enumerate(home):
            result[:, columns] = found[k * local : (k + 1) * local].astype(BF)
    stack(left_out, push[...], hidden[...])
    for at, grad in zip(own_and_other(half), (grad_own, grad_other)):
        stack(left_in, grad[...], rows_in[:, at], at)


def product(left, right, made, result, columns, sem, step):
    copies = []
    for i, (at, size) in enumerate(chunks(left.shape[1], step)):
        made[at : at + size, :] = contract_rows(left[:, at : at + size], right[...]).astype(BF)
        target = result.at[pl.ds(at, size), columns]
        copies.append(pltpu.make_async_copy(made.at[pl.ds(at, size)], target, sem.at[i]))
        copies[-1].start()
    return copies


def out_own_kernel(echo_own, up_own, left, w_out, grad_out, back_own, right, made, sem):
    at_own = own_and_other(echo_own.shape[1])[0]
    stack(right, up_own[...], echo_own[...])
    copies = product(left, right, made, grad_out, at_own, sem, 128)
    back_own[...] = contract_cols(echo_own[...], w_out[:, at_own])
    for copy in copies:
        copy.wait()


def final_kernel(*refs):
    (
        echo_other, up_other, left_out, left_in, back_pre, slope, bend, second, back_hidden, back_own,
        w_out, packed, readout, *home, _, grad_out, grad_in, r2_grad,
        right_out, right_in, made_out, made_in, made_r2, sem_out, sem_in, sem_r2,
    ) = refs
    half = echo_other.shape[1]
    at_own, at_other = own_and_other(half)
    stack(right_out, up_other[...], echo_other[...])
    copies = product(left_out, right_out, made_out, grad_out, at_other, sem_out, 128)
    back = back_own[...] + contract_cols(echo_other[...], w_out[:, at_other])
    final_pre = (back * slope[...] + second[...] * back_hidden[...] * bend[...]).astype(BF)
    stack(right_in, back_pre[...], final_pre)
    copies += product(left_in, right_in, made_in, grad_in, slice(None), sem_in, 256)
    slot = packed[:, 2 * half :].astype(F32)
    slot = slot[:, 1:2] * 128.0 + slot[:, 2:3]
    for columns, at in ((slice(0, half), at_own), (slice(half, 2 * half), at_other)):
        picked = sum(found[:, columns].astype(F32) for found in home)
        tangent = jnp.tanh(packed[:, at].astype(F32))
        dropped = readout[:, at] * (1.0 - tangent * tangent)
        made_r2[:, at] = jnp.where(slot >= 0.0, picked, dropped).astype(BF)
    copies.append(pltpu.make_async_copy(made_r2, r2_grad, sem_r2))
    copies[-1].start()
    for copy in copies:
        copy.wait()


def run(kernel, shapes, args, flops, scratch=(), hbm=(), alias=None):
    spaces = [pl.ANY if at in hbm else pltpu.VMEM for at in range(len(shapes))]
    sources = [pl.ANY if alias and at in alias else pltpu.VMEM for at in range(len(args))]
    return pl.pallas_call(
        kernel,
        out_shape=[jax.ShapeDtypeStruct(shape, kind) for shape, kind in shapes],
        in_specs=[pl.BlockSpec(memory_space=space) for space in sources],
        out_specs=[pl.BlockSpec(memory_space=space) for space in spaces],
        scratch_shapes=list(scratch),
        input_output_aliases=alias or {},
        compiler_params=pltpu.CompilerParams(vmem_limit_bytes=20 << 20),
        cost_estimate=pl.CostEstimate(flops=flops, bytes_accessed=0, transcendentals=0),
    )(*[
        arg if space is pl.ANY else pltpu.with_memory_space_constraint(arg, pltpu.VMEM)
        for arg, space in zip(args, sources)
    ])


def hold(matrix, after):
    def kernel(source, after_ref, held, there, sem):
        del after_ref
        copy = pltpu.make_async_copy(source, held, sem)
        copy.start()
        there[...] = jnp.zeros_like(there)
        copy.wait()

    vmem = pl.BlockSpec(memory_space=pltpu.VMEM)
    return pl.pallas_call(
        kernel,
        out_shape=(pltpu.VMEM(matrix.shape, matrix.dtype), pltpu.VMEM(after.shape, BF)),
        in_specs=[pl.BlockSpec(memory_space=pltpu.HBM), pl.BlockSpec(memory_space=pl.ANY)],
        out_specs=(vmem, vmem),
        scratch_shapes=[pltpu.SemaphoreType.DMA],
        compiler_params=pltpu.CompilerParams(vmem_limit_bytes=1 << 20),
        cost_estimate=pl.CostEstimate(flops=0, bytes_accessed=matrix.size * 4, transcendentals=0),
    )(pltpu.with_memory_space_constraint(matrix, pltpu.HBM), after)


def pack(tokens, combine, routes, capacity_slot):
    local, width = tokens.shape
    shape = (local, width + 128)
    column = lax.broadcasted_iota(jnp.int32, shape, 1) - width
    routes, slots, combine = (
        lax.broadcast_in_dim(values, shape, (0,)) for values in (routes, capacity_slot, combine)
    )
    numbers = jnp.where(column == 4, lax.axis_index("dp"), jnp.where(column == 0, routes, slots))
    numbers = jnp.where(column == 1, numbers >> 7, numbers & 127).astype(BF)
    numbers = jnp.where(column == 3, combine, numbers)
    return jnp.where(column < 0, jnp.pad(tokens, ((0, 0), (0, 128))), numbers)


def shards(tokens, combine, routes, capacity_slot, readout, weight_in, weight_out):
    n_dp = lax.axis_size("dp")
    n_ex = lax.axis_size("expert")
    local, width = tokens.shape
    units = weight_in.shape[2]
    capacity = 5 * local * n_ex // (4 * n_dp)
    rows = n_dp * capacity
    splits = digits(n_ex)
    core, chips = splits[0], splits[1:]

    packed = pack(tokens, combine, routes, capacity_slot)
    first_core = lax.axis_index("expert") % core[1] == 0
    packed, first_core = lax.optimization_barrier((packed, first_core))

    dp_digit = (n_ex, n_dp)
    stages = [[dp_digit]] + pairs(chips) if n_dp > 2 else pairs([dp_digit] + chips)
    stages += [[core]]
    gathered, blocks, (matrix_in, matrix_out) = gather_rows(
        packed,
        stages,
        functools.partial(hold, weight_in[0]),
        functools.partial(hold, weight_out[0]),
    )
    found_at = [blocks.index(((*dp_digit, k),) if k > 0 else ()) * local for k in range(n_dp)]

    half = width // 2
    head_part = jnp.where(first_core, readout[None, :half], readout[None, half:])
    wide, thin, part = (rows, width), (rows, units), (rows, half)
    half_flops = rows * width * units

    def swap(values):
        return fetch(values, [(*core, 1)])

    def shared_sum(mine, other, home=()):
        total = mine + other.astype(F32)
        for stage in pairs(chips):
            own = total.astype(BF)
            last = home and stage == pairs(chips)[-1]
            if last:
                own, *home = lax.optimization_barrier((own, *home))
            parts = [fetch(own, steps_of(stage, offset)) for offset in offsets_of(stage)[1:]]
            if last:
                home[1:] = [fetch(home[k], [(*dp_digit, k)], back=True) for k in range(1, n_dp)]
                parts, home = lax.optimization_barrier((parts, home))
            total = own.astype(F32) + sum(part.astype(F32) for part in parts)
        return (total, *home) if home else total

    rows_in, col, hidden, pre_act, other, picks = run(
        functools.partial(forward_kernel, local, found_at),
        [(wide, BF), ((rows, 1), F32), (thin, BF), (thin, F32), (part, BF),
         ((n_dp * local, rows), F32)],
        (*gathered, matrix_in, matrix_out),
        3 * half_flops,
    )
    other = swap(other)
    mine, slope, bend, col_wide = run(
        mix_kernel,
        [(part, F32), (thin, F32), (thin, F32), (part, F32)],
        (hidden, pre_act, col, matrix_out),
        half_flops,
    )
    mixed = shared_sum(mine, other)
    rows_part = jnp.where(first_core, rows_in[:, :half], rows_in[:, half:])
    tangent = jnp.tanh(rows_part.astype(F32) + mixed)
    sech_sq = 1.0 - tangent * tangent
    upstream = head_part * sech_sq
    up_own = upstream.astype(BF)
    up_other = swap(up_own)
    (back_own,) = run(back_own_kernel, [(thin, F32)], (up_own, matrix_out), half_flops)
    back_hidden, back_pre, other = run(
        backward_kernel,
        [(thin, F32), (thin, BF), (part, BF)],
        (back_own, up_other, col, slope, matrix_in, matrix_out),
        2 * half_flops,
    )
    other = swap(other)
    (mine,) = run(grad_kernel, [(part, F32)], (back_pre, matrix_in), half_flops)
    grad_own = (upstream + shared_sum(mine, other)).astype(BF)
    grad_other = swap(grad_own)
    (second_own,) = run(second_own_kernel, [(thin, F32)], (grad_own, matrix_in), half_flops)
    second, push, other = run(
        push_kernel,
        [(thin, F32), (thin, BF), (part, BF)],
        (second_own, grad_other, col, slope, matrix_in, matrix_out),
        2 * half_flops,
    )
    other = swap(other)
    deep = 2 * padded(rows)
    mine, left_out, left_in, *home = run(
        pull_kernel,
        [(part, F32), ((deep, units), BF), ((deep, width), BF)] + [((local, width), BF)] * n_dp,
        (push, hidden, grad_own, grad_other, rows_in, picks, matrix_out),
        half_flops,
    )
    pushed, *home = shared_sum(mine, other, home)

    total_push = grad_own.astype(F32) + pushed
    curve_term = total_push * head_part * (-2.0 * tangent * sech_sq)
    echo_own = (col_wide * curve_term).astype(BF)
    echo_other = swap(echo_own)
    copies_in, copies_out = (
        pltpu.SemaphoreType.DMA((len(chunks(*size)),)) for size in ((width, 256), (units, 128))
    )
    grad_out, back_own = run(
        out_own_kernel,
        [((units, width), BF), (thin, F32)],
        (echo_own, up_own, left_out, matrix_out),
        2 * half_flops,
        scratch=[
            pltpu.VMEM((deep, half), BF),
            pltpu.VMEM((units, half), BF),
            copies_out,
        ],
        hbm=(0,),
    )
    args = (echo_other, up_other, left_out, left_in, back_pre, slope, bend, second,
            back_hidden, back_own, matrix_out, packed, readout[None, :], *home, grad_out)
    grad_out, grad_in, r2_grad = run(
        final_kernel,
        [((units, width), BF), ((width, units), BF), ((local, width), BF)],
        args,
        4 * half_flops,
        scratch=[
            pltpu.VMEM((deep, half), BF),
            pltpu.VMEM((deep, units), BF),
            pltpu.VMEM((units, half), BF),
            pltpu.VMEM((width, units), BF),
            pltpu.VMEM((local, width), BF),
            copies_out,
            copies_in,
            pltpu.SemaphoreType.DMA,
        ],
        hbm=(0, 1, 2),
        alias={len(args) - 1: 0},
    )

    return (r2_grad, grad_in[None], grad_out[None])


def solution(mesh):
    placed = (
        P(("dp", "expert"), None),
        P(("dp", "expert")),
        P(("dp", "expert")),
        P(("dp", "expert")),
        P(),
        P("dp", None, "expert"),
        P("dp", "expert", None),
    )
    return jax.shard_map(
        shards,
        mesh=mesh,
        in_specs=placed,
        out_specs=(P(("dp", "expert"), None), P("dp", None, "expert"), P("dp", "expert", None)),
        check_vma=False,
    )
```

```python
import functools
import itertools

import jax
import jax.numpy as jnp
from jax import lax
from jax.experimental import pallas as pl
from jax.experimental.pallas import tpu as pltpu
from jax.sharding import PartitionSpec as P

BF = jnp.bfloat16
F32 = jnp.float32


def contract_rows(left, right):
    return lax.dot_general(left, right, (((0,), (0,)), ((), ())), preferred_element_type=F32)


def dot(left, right):
    return jnp.dot(left, right, preferred_element_type=F32)


def digits(total):
    placed, stride = [], 1
    while stride < total:
        size = 2 if total // stride % 2 == 0 else total // stride
        placed.append((stride, size))
        stride *= size
    return placed


def pairs(some):
    return [some[at : at + 2] for at in range(0, len(some), 2)]


def moved(index, stride, size, offset):
    digit = (index // stride) % size
    if size & (size - 1) == 0:
        target = digit ^ offset
    else:
        target = (digit + offset) % size
    return index + (target - digit) * stride


def fetch(values, steps, back=False):
    axes = ("dp", "expert")
    pairs = []
    for here in range(lax.axis_size(axes)):
        there = here
        for stride, size, offset in steps:
            there = moved(there, stride, size, offset)
        pairs.append((here, there) if back else (there, here))
    return lax.ppermute(values, axes, pairs)


def offsets_of(stage):
    return list(itertools.product(*[range(size) for _, size in stage]))


def steps_of(stage, offset):
    return [(*digit, k) for digit, k in zip(stage, offset) if k > 0]


def gather_rows(values, stages, hold_first, hold_second):
    held, blocks, kept = [values], [()], [hold_first(values)]
    for at, stage in enumerate(stages):
        offsets = offsets_of(stage)
        if at == 1:
            held[0] = lax.optimization_barrier(held[0] + kept[0][1])
        if held[0].shape[0] < 8:
            held = [jnp.concatenate(held, axis=0)]
        if at == 1:
            kept.append(hold_second(held[0]))
        if at > 1 and at == len(stages) - 1:
            held[0] = held[0] + kept[1][1]
        held += [fetch(part, steps_of(stage, offset)) for offset in offsets[1:] for part in held]
        blocks = [block + tuple(steps_of(stage, offset)) for offset in offsets for block in blocks]
    return held, blocks, [first for first, _ in kept]


def chunks(total, step):
    return [(at, min(step, total - at)) for at in range(0, total, step)]


def padded(rows):
    return -(-rows // 16) * 16


def stack(ref, low, high, columns=slice(None)):
    rows = low.shape[0]
    space = padded(rows)
    for at, values in ((0, low), (space, high)):
        if space > rows:
            fill = jnp.zeros((space - rows, values.shape[1]), values.dtype)
            values = jnp.concatenate([values, fill], axis=0)
        ref[at : at + space, columns] = values


def own_and_other(size):
    core = lax.rem(lax.axis_index("expert"), 2)
    return tuple(pl.ds(pl.multiple_of(at * size, size), size) for at in (core, 1 - core))


def forward_kernel(local, found_at, *refs):
    *parts, w_in, w_out, rows_in, col, hidden, pre_act, other, picks = refs
    rows, width = rows_in.shape
    gathered = jnp.concatenate([part[...] for part in parts], axis=0)
    meta = gathered[:, width:].astype(F32)
    me = lax.axis_index("dp").astype(F32)
    slot = meta[:, 1:2] * 128.0 + meta[:, 2:3]
    capacity = float(rows // lax.axis_size("dp"))
    place = jnp.where(meta[:, 0:1] == me, meta[:, 4:5] * capacity + slot, -1.0)
    place = jnp.where(slot >= 0.0, place, -1.0)
    wanted = lax.broadcasted_iota(jnp.int32, (meta.shape[0], rows), 1).astype(F32)
    onehot = (place == wanted).astype(F32)
    found = contract_rows(onehot.astype(BF), gathered)
    packed_rows = found[:, :width].astype(BF)
    weight = found[:, width + 3 : width + 4]
    rows_in[...] = packed_rows
    picks[...] = jnp.concatenate([onehot[at : at + local] for at in found_at], axis=0)
    col[...] = weight
    pre = dot(packed_rows, w_in[...])
    pre_act[...] = pre
    act = (pre * jax.nn.sigmoid(pre)).astype(BF)
    hidden[...] = act
    other[...] = (weight * dot(act, w_out[:, own_and_other(width // 2)[1]])).astype(BF)


def mix_kernel(hidden, pre_act, col, w_out, mine, slope, bend, col_wide):
    mine[...] = col[...] * dot(hidden[...], w_out[:, own_and_other(mine.shape[1])[0]])
    pre = pre_act[...]
    sigm = jax.nn.sigmoid(pre)
    slope[...] = sigm * (1.0 + pre * (1.0 - sigm))
    bend[...] = sigm * (1.0 - sigm) * (2.0 + pre * (1.0 - 2.0 * sigm))
    col_wide[...] = jnp.broadcast_to(col[...], col_wide.shape)


def turn_kernel(source, turned):
    for at, size in chunks(source.shape[0], 128):
        turned[:, at : at + size] = source[at : at + size, :].T


def back_own_kernel(up_own, turned_out, back_own):
    back_own[...] = dot(up_own[...], turned_out[own_and_other(up_own.shape[1])[0], :])


def backward_kernel(
    back_own, up_other, col, slope, turned_in, turned_out, back_hidden, back_pre, other
):
    at_other = own_and_other(up_other.shape[1])[1]
    back = col[...] * (back_own[...] + dot(up_other[...], turned_out[at_other, :]))
    back_hidden[...] = back
    back = (back * slope[...]).astype(BF)
    back_pre[...] = back
    other[...] = dot(back, turned_in[:, at_other]).astype(BF)


def grad_kernel(back_pre, turned_in, mine):
    mine[...] = dot(back_pre[...], turned_in[:, own_and_other(mine.shape[1])[0]])


def second_own_kernel(grad_own, w_in, second_own):
    second_own[...] = dot(grad_own[...], w_in[own_and_other(grad_own.shape[1])[0], :])


def push_kernel(second_own, grad_other, col, slope, w_in, w_out, second, push, other):
    at_other = own_and_other(grad_other.shape[1])[1]
    moved_rows = second_own[...] + dot(grad_other[...], w_in[at_other, :])
    second[...] = moved_rows
    moved_rows = (col[...] * moved_rows * slope[...]).astype(BF)
    push[...] = moved_rows
    other[...] = dot(moved_rows, w_out[:, at_other]).astype(BF)


def pull_kernel(
    push, hidden, grad_own, grad_other, rows_in, picks, w_out, mine, left_out, left_in, *home
):
    half = mine.shape[1]
    mine[...] = dot(push[...], w_out[:, own_and_other(half)[0]])
    pick = picks[...].astype(BF)
    local = home[0].shape[0]
    for columns, grad in ((slice(0, half), grad_own), (slice(half, 2 * half), grad_other)):
        found = dot(pick, grad[...])
        for k, result in enumerate(home):
            result[:, columns] = found[k * local : (k + 1) * local].astype(BF)
    stack(left_out, push[...], hidden[...])
    for at, grad in zip(own_and_other(half), (grad_own, grad_other)):
        stack(left_in, grad[...], rows_in[:, at], at)


def product(left, right, made, result, columns, sem, step):
    copies = []
    for i, (at, size) in enumerate(chunks(left.shape[1], step)):
        made[at : at + size, :] = contract_rows(left[:, at : at + size], right[...]).astype(BF)
        target = result.at[pl.ds(at, size), columns]
        copies.append(pltpu.make_async_copy(made.at[pl.ds(at, size)], target, sem.at[i]))
        copies[-1].start()
    return copies


def out_own_kernel(echo_own, up_own, left, turned_out, grad_out, back_own, right, made, sem):
    at_own = own_and_other(echo_own.shape[1])[0]
    stack(right, up_own[...], echo_own[...])
    copies = product(left, right, made, grad_out, at_own, sem, 128)
    back_own[...] = dot(echo_own[...], turned_out[at_own, :])
    for copy in copies:
        copy.wait()


def final_kernel(*refs):
    (
        echo_other, up_other, left_out, left_in, back_pre, slope, bend, second, back_hidden, back_own,
        turned_out, packed, readout, *home, _, grad_out, grad_in, r2_grad,
        right_out, right_in, made_out, made_in, made_r2, sem_out, sem_in, sem_r2,
    ) = refs
    half = echo_other.shape[1]
    at_own, at_other = own_and_other(half)
    stack(right_out, up_other[...], echo_other[...])
    copies = product(left_out, right_out, made_out, grad_out, at_other, sem_out, 128)
    back = back_own[...] + dot(echo_other[...], turned_out[at_other, :])
    final_pre = (back * slope[...] + second[...] * back_hidden[...] * bend[...]).astype(BF)
    stack(right_in, back_pre[...], final_pre)
    copies += product(left_in, right_in, made_in, grad_in, slice(None), sem_in, 256)
    slot = packed[:, 2 * half :].astype(F32)
    slot = slot[:, 1:2] * 128.0 + slot[:, 2:3]
    for columns, at in ((slice(0, half), at_own), (slice(half, 2 * half), at_other)):
        picked = sum(found[:, columns].astype(F32) for found in home)
        tangent = jnp.tanh(packed[:, at].astype(F32))
        dropped = readout[:, at] * (1.0 - tangent * tangent)
        made_r2[:, at] = jnp.where(slot >= 0.0, picked, dropped).astype(BF)
    copies.append(pltpu.make_async_copy(made_r2, r2_grad, sem_r2))
    copies[-1].start()
    for copy in copies:
        copy.wait()


def run(kernel, shapes, args, flops, scratch=(), hbm=(), alias=None, kept=()):
    spaces = [pl.ANY if at in hbm else pltpu.VMEM for at in range(len(shapes))]
    sources = [pl.ANY if alias and at in alias else pltpu.VMEM for at in range(len(args))]
    return pl.pallas_call(
        kernel,
        out_shape=[
            pltpu.VMEM(shape, kind) if at in kept else jax.ShapeDtypeStruct(shape, kind)
            for at, (shape, kind) in enumerate(shapes)
        ],
        in_specs=[pl.BlockSpec(memory_space=space) for space in sources],
        out_specs=[pl.BlockSpec(memory_space=space) for space in spaces],
        scratch_shapes=list(scratch),
        input_output_aliases=alias or {},
        compiler_params=pltpu.CompilerParams(vmem_limit_bytes=20 << 20),
        cost_estimate=pl.CostEstimate(flops=flops, bytes_accessed=0, transcendentals=0),
    )(*[
        arg if space is pl.ANY else pltpu.with_memory_space_constraint(arg, pltpu.VMEM)
        for arg, space in zip(args, sources)
    ])


def hold(matrix, after):
    def kernel(source, after_ref, held, there, sem):
        del after_ref
        copy = pltpu.make_async_copy(source, held, sem)
        copy.start()
        there[...] = jnp.zeros_like(there)
        copy.wait()

    vmem = pl.BlockSpec(memory_space=pltpu.VMEM)
    return pl.pallas_call(
        kernel,
        out_shape=(pltpu.VMEM(matrix.shape, matrix.dtype), pltpu.VMEM(after.shape, BF)),
        in_specs=[pl.BlockSpec(memory_space=pltpu.HBM), pl.BlockSpec(memory_space=pl.ANY)],
        out_specs=(vmem, vmem),
        scratch_shapes=[pltpu.SemaphoreType.DMA],
        compiler_params=pltpu.CompilerParams(vmem_limit_bytes=1 << 20),
        cost_estimate=pl.CostEstimate(flops=0, bytes_accessed=matrix.size * 4, transcendentals=0),
    )(pltpu.with_memory_space_constraint(matrix, pltpu.HBM), after)


def pack(tokens, combine, routes, capacity_slot):
    local, width = tokens.shape
    shape = (local, width + 128)
    column = lax.broadcasted_iota(jnp.int32, shape, 1) - width
    routes, slots, combine = (
        lax.broadcast_in_dim(values, shape, (0,)) for values in (routes, capacity_slot, combine)
    )
    numbers = jnp.where(column == 4, lax.axis_index("dp"), jnp.where(column == 0, routes, slots))
    numbers = jnp.where(column == 1, numbers >> 7, numbers & 127).astype(BF)
    numbers = jnp.where(column == 3, combine, numbers)
    return jnp.where(column < 0, jnp.pad(tokens, ((0, 0), (0, 128))), numbers)


def shards(tokens, combine, routes, capacity_slot, readout, weight_in, weight_out):
    n_dp = lax.axis_size("dp")
    n_ex = lax.axis_size("expert")
    local, width = tokens.shape
    units = weight_in.shape[2]
    capacity = 5 * local * n_ex // (4 * n_dp)
    rows = n_dp * capacity
    splits = digits(n_ex)
    core, chips = splits[0], splits[1:]

    packed = pack(tokens, combine, routes, capacity_slot)
    first_core = lax.axis_index("expert") % core[1] == 0
    packed, first_core = lax.optimization_barrier((packed, first_core))

    dp_digit = (n_ex, n_dp)
    stages = [[dp_digit]] + pairs(chips) if n_dp > 2 else pairs([dp_digit] + chips)
    stages += [[core]]
    gathered, blocks, (matrix_in, matrix_out) = gather_rows(
        packed,
        stages,
        functools.partial(hold, weight_in[0]),
        functools.partial(hold, weight_out[0]),
    )
    found_at = [blocks.index(((*dp_digit, k),) if k > 0 else ()) * local for k in range(n_dp)]

    half = width // 2
    head_part = jnp.where(first_core, readout[None, :half], readout[None, half:])
    wide, thin, part = (rows, width), (rows, units), (rows, half)
    half_flops = rows * width * units

    def swap(values):
        return fetch(values, [(*core, 1)])

    def shared_sum(mine, other, beside=(), home=()):
        total = mine + other.astype(F32)
        for stage in pairs(chips):
            own = total.astype(BF)
            last = stage == pairs(chips)[-1]
            if last and home:
                own, *home = lax.optimization_barrier((own, *home))
            parts = [fetch(own, steps_of(stage, offset)) for offset in offsets_of(stage)[:0:-1]]
            if last and home:
                home[1:] = [fetch(home[k], [(*dp_digit, k)], back=True) for k in range(1, n_dp)]
                beside = home
            if last and beside:
                parts, beside = lax.optimization_barrier((parts, beside))
            total = own.astype(F32) + sum(part.astype(F32) for part in parts)
        return (total, beside) if beside else total

    rows_in, col, hidden, pre_act, other, picks = run(
        functools.partial(forward_kernel, local, found_at),
        [(wide, BF), ((rows, 1), F32), (thin, BF), (thin, F32), (part, BF),
         ((n_dp * local, rows), F32)],
        (*gathered, matrix_in, matrix_out),
        3 * half_flops,
    )
    other = swap(other)
    mine, slope, bend, col_wide = run(
        mix_kernel,
        [(part, F32), (thin, F32), (thin, F32), (part, F32)],
        (hidden, pre_act, col, matrix_out),
        half_flops,
    )
    turned = [
        run(turn_kernel, [(matrix.shape[::-1], BF)], (matrix,), 8 * half_flops, kept=(0,))[0]
        for matrix in (matrix_in, matrix_out)
    ]
    mixed, (turned_in, turned_out) = shared_sum(mine, other, turned)
    rows_part = jnp.where(first_core, rows_in[:, :half], rows_in[:, half:])
    tangent = jnp.tanh(rows_part.astype(F32) + mixed)
    sech_sq = 1.0 - tangent * tangent
    upstream = head_part * sech_sq
    up_own = upstream.astype(BF)
    up_other = swap(up_own)
    (back_own,) = run(back_own_kernel, [(thin, F32)], (up_own, turned_out), half_flops)
    back_hidden, back_pre, other = run(
        backward_kernel,
        [(thin, F32), (thin, BF), (part, BF)],
        (back_own, up_other, col, slope, turned_in, turned_out),
        2 * half_flops,
    )
    other = swap(other)
    (mine,) = run(grad_kernel, [(part, F32)], (back_pre, turned_in), half_flops)
    grad_own = (upstream + shared_sum(mine, other)).astype(BF)
    grad_other = swap(grad_own)
    (second_own,) = run(second_own_kernel, [(thin, F32)], (grad_own, matrix_in), half_flops)
    second, push, other = run(
        push_kernel,
        [(thin, F32), (thin, BF), (part, BF)],
        (second_own, grad_other, col, slope, matrix_in, matrix_out),
        2 * half_flops,
    )
    other = swap(other)
    deep = 2 * padded(rows)
    mine, left_out, left_in, *home = run(
        pull_kernel,
        [(part, F32), ((deep, units), BF), ((deep, width), BF)] + [((local, width), BF)] * n_dp,
        (push, hidden, grad_own, grad_other, rows_in, picks, matrix_out),
        half_flops,
    )
    pushed, home = shared_sum(mine, other, home=home)

    total_push = grad_own.astype(F32) + pushed
    curve_term = total_push * head_part * (-2.0 * tangent * sech_sq)
    echo_own = (col_wide * curve_term).astype(BF)
    echo_other = swap(echo_own)
    copies_in, copies_out = (
        pltpu.SemaphoreType.DMA((len(chunks(*size)),)) for size in ((width, 256), (units, 128))
    )
    grad_out, back_own = run(
        out_own_kernel,
        [((units, width), BF), (thin, F32)],
        (echo_own, up_own, left_out, turned_out),
        2 * half_flops,
        scratch=[
            pltpu.VMEM((deep, half), BF),
            pltpu.VMEM((units, half), BF),
            copies_out,
        ],
        hbm=(0,),
    )
    args = (echo_other, up_other, left_out, left_in, back_pre, slope, bend, second,
            back_hidden, back_own, turned_out, packed, readout[None, :], *home, grad_out)
    grad_out, grad_in, r2_grad = run(
        final_kernel,
        [((units, width), BF), ((width, units), BF), ((local, width), BF)],
        args,
        4 * half_flops,
        scratch=[
            pltpu.VMEM((deep, half), BF),
            pltpu.VMEM((deep, units), BF),
            pltpu.VMEM((units, half), BF),
            pltpu.VMEM((width, units), BF),
            pltpu.VMEM((local, width), BF),
            copies_out,
            copies_in,
            pltpu.SemaphoreType.DMA,
        ],
        hbm=(0, 1, 2),
        alias={len(args) - 1: 0},
    )

    return (r2_grad, grad_in[None], grad_out[None])


def solution(mesh):
    placed = (
        P(("dp", "expert"), None),
        P(("dp", "expert")),
        P(("dp", "expert")),
        P(("dp", "expert")),
        P(),
        P("dp", None, "expert"),
        P("dp", "expert", None),
    )
    return jax.shard_map(
        shards,
        mesh=mesh,
        in_specs=placed,
        out_specs=(P(("dp", "expert"), None), P("dp", None, "expert"), P("dp", "expert", None)),
        check_vma=False,
    )
```

```python
import functools
import itertools

import jax
import jax.numpy as jnp
from jax import lax
from jax.experimental import pallas as pl
from jax.experimental.pallas import tpu as pltpu
from jax.sharding import PartitionSpec as P

BF = jnp.bfloat16
F32 = jnp.float32


def contract_rows(left, right):
    return lax.dot_general(left, right, (((0,), (0,)), ((), ())), preferred_element_type=F32)


def dot(left, right):
    return jnp.dot(left, right, preferred_element_type=F32)


def digits(total):
    placed, stride = [], 1
    while stride < total:
        size = 2 if total // stride % 2 == 0 else total // stride
        placed.append((stride, size))
        stride *= size
    return placed


def pairs(some):
    return [some[at : at + 2] for at in range(0, len(some), 2)]


def moved(index, stride, size, offset):
    digit = (index // stride) % size
    if size & (size - 1) == 0:
        target = digit ^ offset
    else:
        target = (digit + offset) % size
    return index + (target - digit) * stride


def fetch(values, steps, back=False):
    axes = ("dp", "expert")
    pairs = []
    for here in range(lax.axis_size(axes)):
        there = here
        for stride, size, offset in steps:
            there = moved(there, stride, size, offset)
        pairs.append((here, there) if back else (there, here))
    return lax.ppermute(values, axes, pairs)


def offsets_of(stage):
    return list(itertools.product(*[range(size) for _, size in stage]))


def steps_of(stage, offset):
    return [(*digit, k) for digit, k in zip(stage, offset) if k > 0]


def gather_rows(values, stages, hold_first, hold_second):
    held, blocks, kept = [values], [()], [hold_first(values)]
    for at, stage in enumerate(stages):
        offsets = offsets_of(stage)
        if at == 1:
            held[0] = lax.optimization_barrier(held[0] + kept[0][1])
        if held[0].shape[0] < 8:
            held = [jnp.concatenate(held, axis=0)]
        if at == 1:
            kept.append(hold_second(held[0]))
        if at > 1 and at == len(stages) - 1:
            late = min(2, len(held) - 1)
            held[late] = held[late] + kept[1][1]
        held += [fetch(part, steps_of(stage, offset)) for offset in offsets[1:] for part in held]
        blocks = [block + tuple(steps_of(stage, offset)) for offset in offsets for block in blocks]
    return held, blocks, [first for first, _ in kept]


def chunks(total, step):
    return [(at, min(step, total - at)) for at in range(0, total, step)]


def padded(rows):
    return -(-rows // 16) * 16


def stack(ref, low, high, columns=slice(None)):
    rows = low.shape[0]
    space = padded(rows)
    for at, values in ((0, low), (space, high)):
        if space > rows:
            fill = jnp.zeros((space - rows, values.shape[1]), values.dtype)
            values = jnp.concatenate([values, fill], axis=0)
        ref[at : at + space, columns] = values


def own_and_other(size):
    core = lax.rem(lax.axis_index("expert"), 2)
    return tuple(pl.ds(pl.multiple_of(at * size, size), size) for at in (core, 1 - core))


def forward_kernel(local, found_at, *refs):
    *parts, w_in, w_out, rows_in, col, hidden, pre_act, other, picks = refs
    rows, width = rows_in.shape
    gathered = jnp.concatenate([part[...] for part in parts], axis=0)
    meta = gathered[:, width:].astype(F32)
    me = lax.axis_index("dp").astype(F32)
    slot = meta[:, 1:2] * 128.0 + meta[:, 2:3]
    capacity = float(rows // lax.axis_size("dp"))
    place = jnp.where(meta[:, 0:1] == me, meta[:, 4:5] * capacity + slot, -1.0)
    place = jnp.where(slot >= 0.0, place, -1.0)
    wanted = lax.broadcasted_iota(jnp.int32, (meta.shape[0], rows), 1).astype(F32)
    onehot = (place == wanted).astype(F32)
    found = contract_rows(onehot.astype(BF), gathered)
    packed_rows = found[:, :width].astype(BF)
    weight = found[:, width + 3 : width + 4]
    rows_in[...] = packed_rows
    picks[...] = jnp.concatenate([onehot[at : at + local] for at in found_at], axis=0)
    col[...] = weight
    pre = dot(packed_rows, w_in[...])
    pre_act[...] = pre
    act = (pre * jax.nn.sigmoid(pre)).astype(BF)
    hidden[...] = act
    other[...] = (weight * dot(act, w_out[:, own_and_other(width // 2)[1]])).astype(BF)


def mix_kernel(hidden, pre_act, col, w_out, mine, slope, bend, col_wide):
    mine[...] = col[...] * dot(hidden[...], w_out[:, own_and_other(mine.shape[1])[0]])
    pre = pre_act[...]
    sigm = jax.nn.sigmoid(pre)
    slope[...] = sigm * (1.0 + pre * (1.0 - sigm))
    bend[...] = sigm * (1.0 - sigm) * (2.0 + pre * (1.0 - 2.0 * sigm))
    col_wide[...] = jnp.broadcast_to(col[...], col_wide.shape)


def turn_kernel(source, turned):
    for at, size in chunks(source.shape[0], 128):
        turned[:, at : at + size] = source[at : at + size, :].T


def back_own_kernel(up_own, turned_out, back_own):
    back_own[...] = dot(up_own[...], turned_out[own_and_other(up_own.shape[1])[0], :])


def backward_kernel(
    back_own, up_other, col, slope, turned_in, turned_out, back_hidden, back_pre, other
):
    at_other = own_and_other(up_other.shape[1])[1]
    back = col[...] * (back_own[...] + dot(up_other[...], turned_out[at_other, :]))
    back_hidden[...] = back
    back = (back * slope[...]).astype(BF)
    back_pre[...] = back
    other[...] = dot(back, turned_in[:, at_other]).astype(BF)


def grad_kernel(back_pre, turned_in, mine):
    mine[...] = dot(back_pre[...], turned_in[:, own_and_other(mine.shape[1])[0]])


def second_own_kernel(grad_own, w_in, second_own):
    second_own[...] = dot(grad_own[...], w_in[own_and_other(grad_own.shape[1])[0], :])


def push_kernel(second_own, grad_other, col, slope, w_in, w_out, second, push, other):
    at_other = own_and_other(grad_other.shape[1])[1]
    moved_rows = second_own[...] + dot(grad_other[...], w_in[at_other, :])
    second[...] = moved_rows
    moved_rows = (col[...] * moved_rows * slope[...]).astype(BF)
    push[...] = moved_rows
    other[...] = dot(moved_rows, w_out[:, at_other]).astype(BF)


def pull_kernel(
    push, hidden, grad_own, grad_other, rows_in, picks, w_out, mine, left_out, left_in, *home
):
    half = mine.shape[1]
    mine[...] = dot(push[...], w_out[:, own_and_other(half)[0]])
    pick = picks[...].astype(BF)
    local = home[0].shape[0]
    for columns, grad in ((slice(0, half), grad_own), (slice(half, 2 * half), grad_other)):
        found = dot(pick, grad[...])
        for k, result in enumerate(home):
            result[:, columns] = found[k * local : (k + 1) * local].astype(BF)
    stack(left_out, push[...], hidden[...])
    for at, grad in zip(own_and_other(half), (grad_own, grad_other)):
        stack(left_in, grad[...], rows_in[:, at], at)


def product(left, right, made, result, columns, sem, step):
    copies = []
    for i, (at, size) in enumerate(chunks(left.shape[1], step)):
        made[at : at + size, :] = contract_rows(left[:, at : at + size], right[...]).astype(BF)
        target = result.at[pl.ds(at, size), columns]
        copies.append(pltpu.make_async_copy(made.at[pl.ds(at, size)], target, sem.at[i]))
        copies[-1].start()
    return copies


def out_own_kernel(echo_own, up_own, left, turned_out, grad_out, back_own, right, made, sem):
    at_own = own_and_other(echo_own.shape[1])[0]
    stack(right, up_own[...], echo_own[...])
    copies = product(left, right, made, grad_out, at_own, sem, 128)
    back_own[...] = dot(echo_own[...], turned_out[at_own, :])
    for copy in copies:
        copy.wait()


def final_kernel(*refs):
    (
        echo_other, up_other, left_out, left_in, back_pre, slope, bend, second, back_hidden, back_own,
        turned_out, packed, readout, *home, _, grad_out, grad_in, r2_grad,
        right_out, right_in, made_out, made_in, made_r2, sem_out, sem_in, sem_r2,
    ) = refs
    half = echo_other.shape[1]
    at_own, at_other = own_and_other(half)
    stack(right_out, up_other[...], echo_other[...])
    copies = product(left_out, right_out, made_out, grad_out, at_other, sem_out, 128)
    back = back_own[...] + dot(echo_other[...], turned_out[at_other, :])
    final_pre = (back * slope[...] + second[...] * back_hidden[...] * bend[...]).astype(BF)
    stack(right_in, back_pre[...], final_pre)
    slot = packed[:, 2 * half :].astype(F32)
    slot = slot[:, 1:2] * 128.0 + slot[:, 2:3]
    for columns, at in ((slice(0, half), at_own), (slice(half, 2 * half), at_other)):
        picked = sum(found[:, columns].astype(F32) for found in home)
        tangent = jnp.tanh(packed[:, at].astype(F32))
        dropped = readout[:, at] * (1.0 - tangent * tangent)
        made_r2[:, at] = jnp.where(slot >= 0.0, picked, dropped).astype(BF)
    copies.append(pltpu.make_async_copy(made_r2, r2_grad, sem_r2))
    copies[-1].start()
    copies += product(left_in, right_in, made_in, grad_in, slice(None), sem_in, 256)
    for copy in copies:
        copy.wait()


def run(kernel, shapes, args, flops, scratch=(), hbm=(), alias=None, kept=()):
    spaces = [pl.ANY if at in hbm else pltpu.VMEM for at in range(len(shapes))]
    sources = [pl.ANY if alias and at in alias else pltpu.VMEM for at in range(len(args))]
    return pl.pallas_call(
        kernel,
        out_shape=[
            pltpu.VMEM(shape, kind) if at in kept else jax.ShapeDtypeStruct(shape, kind)
            for at, (shape, kind) in enumerate(shapes)
        ],
        in_specs=[pl.BlockSpec(memory_space=space) for space in sources],
        out_specs=[pl.BlockSpec(memory_space=space) for space in spaces],
        scratch_shapes=list(scratch),
        input_output_aliases=alias or {},
        compiler_params=pltpu.CompilerParams(vmem_limit_bytes=20 << 20),
        cost_estimate=pl.CostEstimate(flops=flops, bytes_accessed=0, transcendentals=0),
    )(*[
        arg if space is pl.ANY else pltpu.with_memory_space_constraint(arg, pltpu.VMEM)
        for arg, space in zip(args, sources)
    ])


def hold(matrix, after):
    def kernel(source, after_ref, held, there, sem):
        del after_ref
        copy = pltpu.make_async_copy(source, held, sem)
        copy.start()
        there[...] = jnp.zeros_like(there)
        copy.wait()

    vmem = pl.BlockSpec(memory_space=pltpu.VMEM)
    return pl.pallas_call(
        kernel,
        out_shape=(pltpu.VMEM(matrix.shape, matrix.dtype), pltpu.VMEM(after.shape, BF)),
        in_specs=[pl.BlockSpec(memory_space=pltpu.HBM), pl.BlockSpec(memory_space=pl.ANY)],
        out_specs=(vmem, vmem),
        scratch_shapes=[pltpu.SemaphoreType.DMA],
        compiler_params=pltpu.CompilerParams(vmem_limit_bytes=1 << 20),
        cost_estimate=pl.CostEstimate(flops=0, bytes_accessed=matrix.size * 4, transcendentals=0),
    )(pltpu.with_memory_space_constraint(matrix, pltpu.HBM), after)


def pack(tokens, combine, routes, capacity_slot):
    local, width = tokens.shape
    shape = (local, width + 128)
    column = lax.broadcasted_iota(jnp.int32, shape, 1) - width
    routes, slots, combine = (
        lax.broadcast_in_dim(values, shape, (0,)) for values in (routes, capacity_slot, combine)
    )
    numbers = jnp.where(column == 4, lax.axis_index("dp"), jnp.where(column == 0, routes, slots))
    numbers = jnp.where(column == 1, numbers >> 7, numbers & 127).astype(BF)
    numbers = jnp.where(column == 3, combine, numbers)
    return jnp.where(column < 0, jnp.pad(tokens, ((0, 0), (0, 128))), numbers)


def shards(tokens, combine, routes, capacity_slot, readout, weight_in, weight_out):
    n_dp = lax.axis_size("dp")
    n_ex = lax.axis_size("expert")
    local, width = tokens.shape
    units = weight_in.shape[2]
    capacity = 5 * local * n_ex // (4 * n_dp)
    rows = n_dp * capacity
    splits = digits(n_ex)
    core, chips = splits[0], splits[1:]

    packed = pack(tokens, combine, routes, capacity_slot)
    first_core = lax.axis_index("expert") % core[1] == 0
    packed, first_core = lax.optimization_barrier((packed, first_core))

    dp_digit = (n_ex, n_dp)
    stages = [[dp_digit]] + pairs(chips) if n_dp > 2 else pairs([dp_digit] + chips)
    stages += [[core]]
    gathered, blocks, (matrix_in, matrix_out) = gather_rows(
        packed,
        stages,
        functools.partial(hold, weight_in[0]),
        functools.partial(hold, weight_out[0]),
    )
    found_at = [blocks.index(((*dp_digit, k),) if k > 0 else ()) * local for k in range(n_dp)]

    half = width // 2
    head_part = jnp.where(first_core, readout[None, :half], readout[None, half:])
    wide, thin, part = (rows, width), (rows, units), (rows, half)
    half_flops = rows * width * units

    def swap(values):
        return fetch(values, [(*core, 1)])

    def shared_sum(mine, other, beside=(), home=()):
        total = mine + other.astype(F32)
        for stage in pairs(chips):
            own = total.astype(BF)
            last = stage == pairs(chips)[-1]
            if last and home:
                own, *home = lax.optimization_barrier((own, *home))
            parts = [fetch(own, steps_of(stage, offset)) for offset in offsets_of(stage)[:0:-1]]
            if last and home:
                home[1:] = [fetch(home[k], [(*dp_digit, k)], back=True) for k in range(1, n_dp)]
                beside = home
            if last and beside:
                parts, beside = lax.optimization_barrier((parts, beside))
            total = own.astype(F32) + sum(part.astype(F32) for part in parts)
        return (total, beside) if beside else total

    rows_in, col, hidden, pre_act, other, picks = run(
        functools.partial(forward_kernel, local, found_at),
        [(wide, BF), ((rows, 1), F32), (thin, BF), (thin, F32), (part, BF),
         ((n_dp * local, rows), F32)],
        (*gathered, matrix_in, matrix_out),
        3 * half_flops,
    )
    other = swap(other)
    mine, slope, bend, col_wide = run(
        mix_kernel,
        [(part, F32), (thin, F32), (thin, F32), (part, F32)],
        (hidden, pre_act, col, matrix_out),
        half_flops,
    )
    turned = [
        run(turn_kernel, [(matrix.shape[::-1], BF)], (matrix,), 8 * half_flops, kept=(0,))[0]
        for matrix in (matrix_in, matrix_out)
    ]
    mixed, (turned_in, turned_out) = shared_sum(mine, other, turned)
    rows_part = jnp.where(first_core, rows_in[:, :half], rows_in[:, half:])
    tangent = jnp.tanh(rows_part.astype(F32) + mixed)
    sech_sq = 1.0 - tangent * tangent
    upstream = head_part * sech_sq
    up_own = upstream.astype(BF)
    up_other = swap(up_own)
    (back_own,) = run(back_own_kernel, [(thin, F32)], (up_own, turned_out), half_flops)
    back_hidden, back_pre, other = run(
        backward_kernel,
        [(thin, F32), (thin, BF), (part, BF)],
        (back_own, up_other, col, slope, turned_in, turned_out),
        2 * half_flops,
    )
    other = swap(other)
    (mine,) = run(grad_kernel, [(part, F32)], (back_pre, turned_in), half_flops)
    grad_own = (upstream + shared_sum(mine, other)).astype(BF)
    grad_other = swap(grad_own)
    (second_own,) = run(second_own_kernel, [(thin, F32)], (grad_own, matrix_in), half_flops)
    second, push, other = run(
        push_kernel,
        [(thin, F32), (thin, BF), (part, BF)],
        (second_own, grad_other, col, slope, matrix_in, matrix_out),
        2 * half_flops,
    )
    other = swap(other)
    deep = 2 * padded(rows)
    mine, left_out, left_in, *home = run(
        pull_kernel,
        [(part, F32), ((deep, units), BF), ((deep, width), BF)] + [((local, width), BF)] * n_dp,
        (push, hidden, grad_own, grad_other, rows_in, picks, matrix_out),
        half_flops,
    )
    pushed, home = shared_sum(mine, other, home=home)

    total_push = grad_own.astype(F32) + pushed
    curve_term = total_push * head_part * (-2.0 * tangent * sech_sq)
    echo_own = (col_wide * curve_term).astype(BF)
    echo_other = swap(echo_own)
    copies_in, copies_out = (
        pltpu.SemaphoreType.DMA((len(chunks(*size)),)) for size in ((width, 256), (units, 128))
    )
    grad_out, back_own = run(
        out_own_kernel,
        [((units, width), BF), (thin, F32)],
        (echo_own, up_own, left_out, turned_out),
        2 * half_flops,
        scratch=[
            pltpu.VMEM((deep, half), BF),
            pltpu.VMEM((units, half), BF),
            copies_out,
        ],
        hbm=(0,),
    )
    args = (echo_other, up_other, left_out, left_in, back_pre, slope, bend, second,
            back_hidden, back_own, turned_out, packed, readout[None, :], *home, grad_out)
    grad_out, grad_in, r2_grad = run(
        final_kernel,
        [((units, width), BF), ((width, units), BF), ((local, width), BF)],
        args,
        4 * half_flops,
        scratch=[
            pltpu.VMEM((deep, half), BF),
            pltpu.VMEM((deep, units), BF),
            pltpu.VMEM((units, half), BF),
            pltpu.VMEM((width, units), BF),
            pltpu.VMEM((local, width), BF),
            copies_out,
            copies_in,
            pltpu.SemaphoreType.DMA,
        ],
        hbm=(0, 1, 2),
        alias={len(args) - 1: 0},
    )

    return (r2_grad, grad_in[None], grad_out[None])


def solution(mesh):
    placed = (
        P(("dp", "expert"), None),
        P(("dp", "expert")),
        P(("dp", "expert")),
        P(("dp", "expert")),
        P(),
        P("dp", None, "expert"),
        P("dp", "expert", None),
    )
    return jax.shard_map(
        shards,
        mesh=mesh,
        in_specs=placed,
        out_specs=(P(("dp", "expert"), None), P("dp", None, "expert"), P("dp", "expert", None)),
        check_vma=False,
    )
```
